32 devices in a mesh: tm: 2 (over x), lat: 8 (over z, y), lon: 2 (over core).
Axes of the slice: x: 2, y: 2, z: 4, core: 2. Of those that a mesh axis runs over, the one named last changes fastest.
Arguments:
- control: bfloat16 [1024, 2, 4, 8, 2048], P('lat', 'tm', None, None, 'lon'), may hold values from -6 to 6
- deviations: float32 [1024, 2, 4, 8, 2048], P('lat', 'tm', None, None, 'lon'), may hold values from 0.3 to 3
- increments: float32 [1024, 2, 4, 8, 2048], P('lat', 'tm', None, None, 'lon'), may hold values from -6 to 6
- lon_corr: bfloat16 [2048, 2048], P('lon'), may hold values from -0.125 to 0.125
- lat_corr: bfloat16 [1024, 1024], P('lat'), may hold values from -0.1875 to 0.1875
- offsets: int32 [2, 8], replicated, may hold values from -2 to 2, as said below
- courant: float32 [4], replicated, may hold values from 0.2 to 0.8
Outputs:
- misfit: float32 [1024, 2, 4, 8, 2048], P('lat', 'tm', None, None, 'lon')
The draws below stay inside these ranges and needn't reach their ends.
Inputs may be any that keep to these rules, and one draw needn't show every extreme that they name: `offsets`: each of the two rows holds both -2 and 2.
All inputs are finite; a program needn't handle non-finite values.
Results may differ from the reference program's by a relative error of at most 0.0024.
Values may be sent and summed in bfloat16 or wider, within the bound.
A program may use at most 256 MiB of HBM per device.

```python
import math
import jax
import jax.numpy as jnp
from jax import lax

NLAT = 1024
NLON = 2048
LEV = 8
NVAR = 4
TSLOTS = 2


def draw_offsets(key, part):
    subkeys = jax.random.split(jax.random.fold_in(key, 7), 2)
    values_drawn = jax.random.randint(subkeys[0], (2, LEV), -2, 3)
    offset_rows = []
    for which_dim in range(2):
        ordering = jax.random.permutation(jax.random.fold_in(subkeys[1], which_dim), LEV)
        offset_row = values_drawn[which_dim].at[ordering[0]].set(-2).at[ordering[1]].set(2)
        offset_rows.append(offset_row)
    return jnp.stack(offset_rows, axis=0).astype(jnp.int32)


def steps_of(own_key, dims, pieces, low, largest):
    factor_of = 1.0
    for axis_at, blocks in pieces:
        heights = jax.random.uniform(jax.random.fold_in(jax.random.fold_in(own_key, 6), axis_at), (blocks,), jnp.float32, low / len(pieces), largest / len(pieces))
        factor_of = factor_of * jnp.repeat(jnp.exp(heights), dims[axis_at] // blocks).reshape((-1,) + (1,) * (len(dims) - 1 - axis_at))
    return factor_of


def bell_draw(rng, dims, width, limit, cuts=(), dtype=jnp.bfloat16):
    entries = jax.random.normal(rng, dims, jnp.float32) * width
    if len(cuts) > 0:
        entries = steps_of(rng, dims, cuts, -0.22, 0.18) * entries
    return jnp.clip(entries, min=-limit, max=limit).astype(dtype)


def setup_inputs(seed: int = 0) -> dict:
    arg_keys = jax.random.split(jax.random.key(seed), 8)
    control = bell_draw(arg_keys[0], (NLAT, TSLOTS, NVAR, LEV, NLON), 1.0, 6.0, ((0, 8), (1, 2), (4, 2)))
    deviations = jnp.clip(jnp.exp(math.log(3.0) - 2.3025851 * jax.random.uniform(arg_keys[1], (NLAT, TSLOTS, NVAR, LEV, NLON), jnp.float32) ** steps_of(arg_keys[1], (NLAT, TSLOTS, NVAR, LEV, NLON), ((0, 8), (1, 2), (4, 2)), -0.2, 0.2)), 0.3, 3.0)
    increments = bell_draw(arg_keys[2], (NLAT, TSLOTS, NVAR, LEV, NLON), 1.0, 6.0, ((0, 8), (1, 2), (4, 2)), jnp.float32)
    lon_corr = bell_draw(arg_keys[3], (NLON, NLON), NLON ** -0.5, 0.125, ((0, 2),))
    lat_corr = bell_draw(arg_keys[4], (NLAT, NLAT), NLAT ** -0.5, 0.1875, ((0, 8),))
    offsets = draw_offsets(jax.random.fold_in(arg_keys[7], 71), 0)
    courant = jnp.clip(jax.random.uniform(arg_keys[6], (NVAR,), jnp.float32, 0.2, 0.8), 0.2, 0.8)
    return dict(control=control, deviations=deviations, increments=increments, lon_corr=lon_corr, lat_corr=lat_corr, offsets=offsets, courant=courant)


def advect(field_now, offsets, courant):
    padded = jnp.pad(field_now, ((2, 2), (0, 0), (0, 0), (0, 0), (0, 0)))
    padded = jnp.concatenate([padded[..., -2:], padded, padded[..., :2]], axis=4)
    displaced_all = []
    for level_idx in range(LEV):
        one_level = padded[:, :, :, level_idx, :]
        displaced = lax.dynamic_slice_in_dim(one_level, (2 - offsets[0, level_idx]).astype(jnp.int32), NLAT, 0)
        displaced = lax.dynamic_slice_in_dim(displaced, (2 - offsets[1, level_idx]).astype(jnp.int32), NLON, 3)
        displaced_all.append(displaced)
    shifted = jnp.stack(displaced_all, axis=3)
    blending = courant.reshape(1, 1, -1, 1, 1)
    return (1.0 - blending) * field_now + blending * shifted


def reference(control, deviations, increments, lon_corr, lat_corr, offsets, courant):
    flat_rows = control.reshape(-1, NLON)
    smoothed = lax.dot_general(flat_rows, lon_corr, (((1,), (1,)), ((), ())), preferred_element_type=jnp.float32)
    halfway = smoothed.astype(jnp.bfloat16).reshape(NLAT, -1)
    correlated = jnp.dot(lat_corr, halfway, preferred_element_type=jnp.float32)
    forcing = deviations * correlated.reshape(control.shape)
    evolved = advect(increments, offsets, courant)
    previous = jnp.concatenate([jnp.zeros_like(evolved[:, :1]), evolved[:, :-1]], axis=1)
    return increments - previous - forcing
```

```python
import jax
import jax.numpy as jnp
from jax import lax
from jax.experimental import pallas as pl
from jax.experimental.pallas import tpu as pltpu
from jax.sharding import PartitionSpec as P


def with_halo(block, sides, width, periodic):
    for axis, dim in sides:
        count = lax.axis_size(axis)
        forward = [(i, i + 1) for i in range(count - 1)]
        if periodic:
            forward.append((count - 1, 0))
        backward = [(target, source) for source, target in forward]
        low = lax.ppermute(
            lax.slice_in_dim(block, block.shape[dim] - width, None, axis=dim), axis, forward
        )
        high = lax.ppermute(lax.slice_in_dim(block, 0, width, axis=dim), axis, backward)
        block = jnp.concatenate([low, block, high], axis=dim)
    return block


def from_behind(value, axis, steps):
    count = lax.axis_size(axis)
    initial, last = (max(0, -steps), min(count, count - steps))
    return lax.ppermute(value, axis, [(source, source + steps) for source in range(initial, last)])


def advect(field_now, offsets, courant):
    widened = with_halo(field_now.astype(jnp.bfloat16), (("lon", 4),), 2, True).astype(
        field_now.dtype
    )
    padded = with_halo(widened.astype(jnp.bfloat16), (("lat", 0),), 2, False).astype(widened.dtype)
    lat_count = field_now.shape[0]
    lon_count = field_now.shape[4]
    displaced_all = []
    for level_idx in range(field_now.shape[3]):
        one_level = padded[:, :, :, level_idx, :]
        displaced = lax.dynamic_slice_in_dim(one_level, 2 - offsets[0, level_idx], lat_count, 0)
        displaced = lax.dynamic_slice_in_dim(displaced, 2 - offsets[1, level_idx], lon_count, 3)
        displaced_all.append(displaced)
    shifted = jnp.stack(displaced_all, axis=3)
    blending = courant.reshape(1, 1, -1, 1, 1)
    return (1.0 - blending) * field_now + blending * shifted


def lat_columns(control, deviations, increments, lon_corr, lat_corr, offsets, courant):
    lat_count = control.shape[0]
    lon_count = control.shape[4]
    flat_rows = control.reshape(-1, lon_count)
    smoothed = lax.dot_general(
        lax.all_gather(flat_rows, "lon", axis=1, tiled=True),
        lon_corr,
        (((1,), (1,)), ((), ())),
        preferred_element_type=jnp.float32,
    )
    halfway = smoothed.astype(jnp.bfloat16).reshape(lat_count, -1)
    full_table = lax.all_gather(lat_corr, "lat", axis=0, tiled=True)
    columns_all = lax.all_to_all(halfway, "lat", split_axis=1, concat_axis=0, tiled=True)
    product = jnp.dot(full_table, columns_all, preferred_element_type=jnp.float32)
    correlated = lax.all_to_all(product, "lat", split_axis=0, concat_axis=1, tiled=True)
    forcing = deviations * correlated.reshape(control.shape)
    evolved = advect(increments, offsets, courant)
    carried = from_behind(evolved, "tm", 1)
    previous = jnp.concatenate([carried, evolved[:, :-1]], axis=1)
    return increments - previous - forcing


LIMIT = 48 * 1024 * 1024


def cost(flops, nbytes):
    return pl.CostEstimate(flops=flops, bytes_accessed=nbytes, transcendentals=0)


def row_block(rows, largest):
    block = min(rows, largest)
    while rows % block:
        block -= 16
    return block


def fields_first(control, first, count):
    rows, nvar, levels, lons = control.shape
    block = row_block(rows, 64)

    def kernel(x_ref, y_ref):
        y_ref[0] = jnp.swapaxes(x_ref[:, 0].astype(jnp.float32), 0, 1).astype(jnp.bfloat16)

    return pl.pallas_call(
        kernel,
        grid=(count, rows // block),
        in_specs=[pl.BlockSpec((block, 1, levels, lons), lambda v, r: (r, first + v, 0, 0))],
        out_specs=pl.BlockSpec((1, levels, block, lons), lambda v, r: (v, 0, r, 0)),
        out_shape=jax.ShapeDtypeStruct((count, levels, rows, lons), jnp.bfloat16),
        compiler_params=pltpu.CompilerParams(vmem_limit_bytes=LIMIT),
        cost_estimate=cost(0, 4 * count * levels * rows * lons),
        name="fields_first",
    )(control)


def evolve(increments, padded, offsets, courant):
    rows, nvar, levels, lons = increments.shape
    wide = padded.shape[-1]
    rim = (wide - lons) // 2
    block = row_block(rows, 32)

    def kernel(off_ref, cour_ref, inc_ref, pad_ref, out_ref):
        weight = cour_ref[pl.program_id(0)]
        start = pl.program_id(1) * block
        lat_off, lon_off = off_ref[:, 0:1], off_ref[:, 1:2]

        def one(i, carry):
            row = jnp.zeros((levels, wide), jnp.float32)
            for step in range(-2, 3):
                source = pad_ref[start + i + 2 - step, 0].astype(jnp.float32)
                row = jnp.where(lat_off == step, source, row)
            moved = jnp.zeros((levels, lons), jnp.float32)
            for step in range(-2, 3):
                rolled = pltpu.roll(row, step % wide, 1) if step else row
                moved = jnp.where(lon_off == step, rolled[:, rim : rim + lons], moved)
            mixed = (1.0 - weight) * inc_ref[i, 0] + weight * moved
            out_ref[i, 0] = mixed.astype(jnp.bfloat16)
            return carry

        lax.fori_loop(0, block, one, 0)

    return pl.pallas_call(
        kernel,
        grid=(nvar, rows // block),
        in_specs=[
            pl.BlockSpec((levels, 2), lambda v, r: (0, 0)),
            pl.BlockSpec(memory_space=pltpu.SMEM),
            pl.BlockSpec((block, 1, levels, lons), lambda v, r: (r, v, 0, 0)),
            pl.BlockSpec((rows + 4, 1, levels, wide), lambda v, r: (0, v, 0, 0)),
        ],
        out_specs=pl.BlockSpec((block, 1, levels, lons), lambda v, r: (r, v, 0, 0)),
        out_shape=jax.ShapeDtypeStruct(increments.shape, jnp.bfloat16),
        compiler_params=pltpu.CompilerParams(vmem_limit_bytes=LIMIT),
        cost_estimate=cost(30 * increments.size, 8 * increments.size),
        name="evolve",
    )(offsets.T, courant, increments, padded)


def residual(increments, deviations, previous, correlated, first, count, filled):
    rows, nvar, levels, lons = increments.shape
    block = row_block(rows, 32)

    def kernel(inc_ref, dev_ref, prev_ref, corr_ref, *others):
        out_ref = others[-1]
        corr = jnp.swapaxes(corr_ref[0].astype(jnp.float32), 0, 1)
        out_ref[:, 0] = (
            inc_ref[:, 0] - prev_ref[:, 0].astype(jnp.float32) - dev_ref[:, 0] * corr
        )

    spec = pl.BlockSpec((block, 1, levels, lons), lambda v, r: (r, first + v, 0, 0))
    in_specs = [spec] * 3 + [
        pl.BlockSpec((1, levels, block, lons), lambda v, r: (v, 0, r, 0))
    ]
    operands = [increments, deviations, previous, correlated]
    aliases = {}
    if filled is not None:
        in_specs.append(pl.BlockSpec(memory_space=pl.ANY))
        operands.append(filled)
        aliases = {4: 0}
    return pl.pallas_call(
        kernel,
        grid=(count, rows // block),
        in_specs=in_specs,
        out_specs=spec,
        out_shape=jax.ShapeDtypeStruct(increments.shape, jnp.float32),
        input_output_aliases=aliases,
        compiler_params=pltpu.CompilerParams(vmem_limit_bytes=LIMIT),
        cost_estimate=cost(6 * count * levels * rows * lons, 16 * count * levels * rows * lons),
        name="residual",
    )(*operands)


def swap(value, axis, steps, periodic):
    count = lax.axis_size(axis)
    pairs = [(i, i + steps) for i in range(count) if 0 <= i + steps < count]
    if periodic:
        pairs = [(i, (i + steps) % count) for i in range(count)]
    return lax.ppermute(value, axis, pairs)


def widen(field, rim):
    lons = field.shape[-1]
    low = swap(field[..., lons - rim :], "lon", 1, True)
    high = swap(field[..., :rim], "lon", -1, True)
    wide = jnp.concatenate([low, field, high], axis=-1)
    below = swap(wide[-2:], "lat", 1, False)
    above = swap(wide[:2], "lat", -1, False)
    return jnp.concatenate([below, wide, above], axis=0)


def gathered_table(lat_corr):
    sharers = lax.axis_size("tm") * lax.axis_size("lon")
    width = lat_corr.shape[1] // sharers
    mine = lax.axis_index("tm") * lax.axis_size("lon") + lax.axis_index("lon")
    piece = lax.dynamic_slice_in_dim(lat_corr, mine * width, width, 1)
    piece = lax.all_gather(piece, "lat", axis=0, tiled=True)
    return lax.all_gather(piece, ("tm", "lon"), axis=1, tiled=True)


def whole_fields(control, deviations, increments, lon_corr, lat_corr, offsets, courant):
    rows, _, nvar, levels, lons = control.shape
    n_lat, n_lon = lax.axis_size("lat"), lax.axis_size("lon")
    group = n_lat * n_lon
    rounds = nvar * levels // group
    vars_each = nvar // rounds
    flat = (rows, nvar, levels, lons)
    control, deviations, increments = (
        x.reshape(flat) for x in (control, deviations, increments)
    )
    sent = []
    for k in range(rounds):
        block = fields_first(control, k * vars_each, vars_each).reshape(group, rows, lons)
        sent.append(
            lax.all_to_all(block, ("lat", "lon"), split_axis=0, concat_axis=0, tiled=True)
        )
    full_lon = lax.all_gather(lon_corr, "lon", axis=0, tiled=True)
    full_lat = gathered_table(lat_corr)
    padded = widen(increments.astype(jnp.bfloat16), 128)
    evolved = evolve(increments, padded, offsets, courant)
    previous = lax.ppermute(evolved, "tm", [(i, i + 1) for i in range(lax.axis_size("tm") - 1)])
    back = []
    for k in range(rounds):
        field = sent[k].reshape(n_lat, n_lon, rows, lons).transpose(0, 2, 1, 3)
        field = field.reshape(n_lat * rows, n_lon * lons)
        smoothed = lax.dot_general(
            field, full_lon, (((1,), (1,)), ((), ())), preferred_element_type=jnp.float32
        ).astype(jnp.bfloat16)
        product = jnp.dot(full_lat, smoothed, preferred_element_type=jnp.float32)
        product = product.astype(jnp.bfloat16).reshape(n_lat, rows, n_lon, lons)
        product = product.transpose(0, 2, 1, 3).reshape(group, rows, lons)
        back.append(
            lax.all_to_all(product, ("lat", "lon"), split_axis=0, concat_axis=0, tiled=True)
        )
    out = None
    for k in range(rounds):
        correlated = back[k].reshape(vars_each, levels, rows, lons)
        out = residual(
            increments, deviations, previous, correlated, k * vars_each, vars_each, out
        )
    return out.reshape(rows, 1, nvar, levels, lons)


def body(control, deviations, increments, lon_corr, lat_corr, offsets, courant):
    rows, slots, nvar, levels, lons = control.shape
    group = lax.axis_size("lat") * lax.axis_size("lon")
    sharers = lax.axis_size("tm") * lax.axis_size("lon")
    arrays = (control, deviations, increments, lon_corr, lat_corr, offsets, courant)
    fits = (
        slots == 1
        and (nvar * levels) % group == 0
        and group % levels == 0
        and rows % 16 == 0
        and lons % 128 == 0
        and lat_corr.shape[1] % (128 * sharers) == 0
    )
    return whole_fields(*arrays) if fits else lat_columns(*arrays)


def solution(mesh):
    in_specs = (
        P("lat", "tm", None, None, "lon"),
        P("lat", "tm", None, None, "lon"),
        P("lat", "tm", None, None, "lon"),
        P("lon", None),
        P("lat", None),
        P(),
        P(),
    )
    out_specs = P("lat", "tm", None, None, "lon")
    return jax.shard_map(body, mesh=mesh, in_specs=in_specs, out_specs=out_specs, check_vma=False)
```

```python
import jax
import jax.numpy as jnp
from jax import lax
from jax.experimental import pallas as pl
from jax.experimental.pallas import tpu as pltpu
from jax.sharding import PartitionSpec as P


def with_halo(block, sides, width, periodic):
    for axis, dim in sides:
        count = lax.axis_size(axis)
        forward = [(i, i + 1) for i in range(count - 1)]
        if periodic:
            forward.append((count - 1, 0))
        backward = [(target, source) for source, target in forward]
        low = lax.ppermute(
            lax.slice_in_dim(block, block.shape[dim] - width, None, axis=dim), axis, forward
        )
        high = lax.ppermute(lax.slice_in_dim(block, 0, width, axis=dim), axis, backward)
        block = jnp.concatenate([low, block, high], axis=dim)
    return block


def from_behind(value, axis, steps):
    count = lax.axis_size(axis)
    initial, last = (max(0, -steps), min(count, count - steps))
    return lax.ppermute(value, axis, [(source, source + steps) for source in range(initial, last)])


def advect(field_now, offsets, courant):
    widened = with_halo(field_now.astype(jnp.bfloat16), (("lon", 4),), 2, True).astype(
        field_now.dtype
    )
    padded = with_halo(widened.astype(jnp.bfloat16), (("lat", 0),), 2, False).astype(widened.dtype)
    lat_count = field_now.shape[0]
    lon_count = field_now.shape[4]
    displaced_all = []
    for level_idx in range(field_now.shape[3]):
        one_level = padded[:, :, :, level_idx, :]
        displaced = lax.dynamic_slice_in_dim(one_level, 2 - offsets[0, level_idx], lat_count, 0)
        displaced = lax.dynamic_slice_in_dim(displaced, 2 - offsets[1, level_idx], lon_count, 3)
        displaced_all.append(displaced)
    shifted = jnp.stack(displaced_all, axis=3)
    blending = courant.reshape(1, 1, -1, 1, 1)
    return (1.0 - blending) * field_now + blending * shifted


def lat_columns(control, deviations, increments, lon_corr, lat_corr, offsets, courant):
    lat_count = control.shape[0]
    lon_count = control.shape[4]
    flat_rows = control.reshape(-1, lon_count)
    smoothed = lax.dot_general(
        lax.all_gather(flat_rows, "lon", axis=1, tiled=True),
        lon_corr,
        (((1,), (1,)), ((), ())),
        preferred_element_type=jnp.float32,
    )
    halfway = smoothed.astype(jnp.bfloat16).reshape(lat_count, -1)
    full_table = lax.all_gather(lat_corr, "lat", axis=0, tiled=True)
    columns_all = lax.all_to_all(halfway, "lat", split_axis=1, concat_axis=0, tiled=True)
    product = jnp.dot(full_table, columns_all, preferred_element_type=jnp.float32)
    correlated = lax.all_to_all(product, "lat", split_axis=0, concat_axis=1, tiled=True)
    forcing = deviations * correlated.reshape(control.shape)
    evolved = advect(increments, offsets, courant)
    carried = from_behind(evolved, "tm", 1)
    previous = jnp.concatenate([carried, evolved[:, :-1]], axis=1)
    return increments - previous - forcing


LIMIT = 60 * 1024 * 1024


def cost(flops, nbytes):
    return pl.CostEstimate(flops=flops, bytes_accessed=nbytes, transcendentals=0)


def row_block(rows, largest):
    block = min(rows, largest)
    while rows % block:
        block -= 16
    return block


def residual(increments, deviations, previous, correlated, first, count, filled):
    rows, nvar, levels, lons = increments.shape
    block = row_block(rows, 32)

    def kernel(inc_ref, dev_ref, prev_ref, corr_ref, *others):
        out_ref = others[-1]
        corr = jnp.swapaxes(corr_ref[0].astype(jnp.float32), 0, 1)
        has_past = lax.axis_index("tm") > 0
        previous = jnp.where(has_past, prev_ref[:, 0].astype(jnp.float32), 0.0)
        out_ref[:, 0] = (
            inc_ref[:, 0] - previous - dev_ref[:, 0] * corr
        )

    spec = pl.BlockSpec((block, 1, levels, lons), lambda v, r: (r, first + v, 0, 0))
    in_specs = [spec] * 3 + [
        pl.BlockSpec((1, levels, block, lons), lambda v, r: (v, 0, r, 0))
    ]
    operands = [increments, deviations, previous, correlated]
    aliases = {}
    if filled is not None:
        in_specs.append(pl.BlockSpec(memory_space=pl.ANY))
        operands.append(filled)
        aliases = {4: 0}
    return pl.pallas_call(
        kernel,
        grid=(count, rows // block),
        in_specs=in_specs,
        out_specs=spec,
        out_shape=jax.ShapeDtypeStruct(increments.shape, jnp.float32),
        input_output_aliases=aliases,
        compiler_params=pltpu.CompilerParams(vmem_limit_bytes=LIMIT),
        cost_estimate=cost(6 * count * levels * rows * lons, 16 * count * levels * rows * lons),
        name="residual",
    )(*operands)


def swap(value, axis, steps, periodic):
    count = lax.axis_size(axis)
    pairs = [(i, i + steps) for i in range(count) if 0 <= i + steps < count]
    if periodic:
        pairs = [(i, (i + steps) % count) for i in range(count)]
    return lax.ppermute(value, axis, pairs)


def widen(field, rim):
    low = swap(field[..., field.shape[-1] - rim :], "lon", 1, True)
    high = swap(field[..., :rim], "lon", -1, True)
    last = jnp.concatenate([low[-2:], field[-2:], high[-2:]], axis=-1)
    first = jnp.concatenate([low[:2], field[:2], high[:2]], axis=-1)
    return low, high, swap(last, "lat", 1, False), swap(first, "lat", -1, False)

def exchange(control, increments, low, high, below, above, lon_corr, lat_corr, offsets, courant):
    rows, nvar, levels, lons = control.shape
    n_tm, n_lat, n_lon = (lax.axis_size(axis) for axis in ("tm", "lat", "lon"))
    group = n_lat * n_lon
    rounds = nvar * levels // group
    vars_each = nvar // rounds
    lats, width = n_lat * rows, n_lon * lons
    rim = low.shape[-1]
    wide = lons + 2 * rim
    strip = lat_corr.shape[1] // (n_tm * n_lon)
    row_tile = row_block(lats, 256)
    lon_tile = row_block(width, 512)
    bf16 = jnp.bfloat16

    def kernel(
        off_ref, cour_ref, ctl, inc, low_ref, high_ref, below_ref, above_ref, lonc, latc,
        corr, prev,
        stage, ctl_buf, whole, table, lat_table, smooth, pad, moved_buf,
        load_sem, self_sem, lon_send, lon_recv, lat_send, lat_recv, tab_send, tab_recv,
        out_send, out_recv, back_send, back_recv, tm_send, tm_recv,
    ):
        tm, la, lo = (lax.axis_index(axis) for axis in ("tm", "lat", "lon"))
        me = la * n_lon + lo
        strip_at = (tm * n_lon + lo) * strip

        def at(index, size):
            return pl.ds(pl.multiple_of(index * size, size), size)

        def remote(src, dst, send, recv, tm_to, lat_to, lon_to):
            return pltpu.make_async_remote_copy(
                src_ref=src, dst_ref=dst, send_sem=send, recv_sem=recv,
                device_id=(tm_to, lat_to, lon_to), device_id_type=pl.DeviceIdType.MESH,
            )

        def each_other(count, mine, do):
            def step(i, carry):
                pl.when(i != mine)(lambda: do(i))
                return carry

            lax.fori_loop(0, count, step, 0)

        barrier = pltpu.get_barrier_semaphore()

        def greet(tm_to, peer):
            pl.semaphore_signal(
                barrier, inc=1, device_id=(tm_to, peer // n_lon, peer % n_lon),
                device_id_type=pl.DeviceIdType.MESH,
            )

        each_other(group, me, lambda peer: greet(tm, peer))
        for lon_to in range(n_lon):
            each_other(n_tm, tm, lambda other: greet(other, la * n_lon + lon_to))
        pl.semaphore_wait(barrier, group - 1 + (n_tm - 1) * n_lon)

        def outward(k, peer, origin):
            return remote(
                stage.at[k * group + peer],
                whole.at[k, at(origin // n_lon, rows), at(origin % n_lon, lons)],
                out_send.at[k, peer], out_recv.at[k, origin],
                tm, peer // n_lon, peer % n_lon,
            )

        def homeward(k, peer, origin):
            return remote(
                whole.at[k, at(peer // n_lon, rows), at(peer % n_lon, lons)],
                corr.at[k * group + origin],
                back_send.at[k, peer], back_recv.at[k, origin],
                tm, peer // n_lon, peer % n_lon,
            )

        def lon_share(lon_to, origin):
            return remote(
                lonc, table.at[at(origin, lons)],
                lon_send.at[lon_to], lon_recv.at[origin], tm, la, lon_to,
            )

        def lat_share(lat_to, origin):
            columns = at(tm * n_lon + lo, strip)
            return remote(
                latc.at[:, columns], lat_table.at[at(origin, rows), columns],
                lat_send.at[lat_to], lat_recv.at[origin], tm, lat_to, lo,
            )

        def strip_share(other, origin):
            return remote(
                lat_table.at[:, at(tm * n_lon + lo, strip)],
                lat_table.at[:, at(tm * n_lon + lo, strip)],
                tab_send.at[other], tab_recv.at[origin], other // n_lon, la, other % n_lon,
            )

        def strip_arrival(origin):
            return remote(
                lat_table.at[:, at(origin, strip)], lat_table.at[:, at(origin, strip)],
                tab_send.at[origin], tab_recv.at[origin], origin // n_lon, la, origin % n_lon,
            )

        def own(k):
            return pltpu.make_async_copy(
                stage.at[k * group + me], whole.at[k, at(la, rows), at(lo, lons)],
                self_sem.at[k],
            )

        def own_back(k):
            return pltpu.make_async_copy(
                whole.at[k, at(la, rows), at(lo, lons)], corr.at[k * group + me],
                self_sem.at[rounds + k],
            )

        def own_tables():
            columns = at(tm * n_lon + lo, strip)
            return (
                pltpu.make_async_copy(lonc, table.at[at(lo, lons)], load_sem.at[0]),
                pltpu.make_async_copy(
                    latc.at[:, columns], lat_table.at[at(la, rows), columns], load_sem.at[1]
                ),
            )

        def send_out(k):
            far = (me * vars_each // group + vars_each // 2) % vars_each
            for t in range(vars_each):
                local = (far + t) % vars_each
                load = pltpu.make_async_copy(
                    ctl.at[:, k * vars_each + local], ctl_buf, load_sem.at[2]
                )
                load.start()
                load.wait()

                def turn(r, carry):
                    part = ctl_buf[pl.ds(r * 16, 16)].astype(jnp.float32)
                    first = (k * vars_each + local) * levels
                    stage[pl.ds(first, levels), pl.ds(r * 16, 16), :] = jnp.swapaxes(
                        part, 0, 1
                    ).astype(bf16)
                    return carry

                lax.fori_loop(0, rows // 16, turn, 0)

                def send(l, carry):
                    peer = local * levels + l
                    pl.when(peer != me)(lambda: outward(k, peer, me).start())
                    return carry

                lax.fori_loop(0, levels, send, 0)
            own(k).start()

        def advect(v):
            body_rows = pl.ds(2, rows)
            loads = [
                pltpu.make_async_copy(
                    inc.at[:, v], pad.at[body_rows, :, pl.ds(rim, lons)], load_sem.at[3]
                ),
                pltpu.make_async_copy(
                    low_ref.at[:, v], pad.at[body_rows, :, pl.ds(0, rim)], load_sem.at[4]
                ),
                pltpu.make_async_copy(
                    high_ref.at[:, v], pad.at[body_rows, :, pl.ds(rim + lons, rim)],
                    load_sem.at[5],
                ),
                pltpu.make_async_copy(below_ref.at[:, v], pad.at[pl.ds(0, 2)], load_sem.at[6]),
                pltpu.make_async_copy(
                    above_ref.at[:, v], pad.at[pl.ds(2 + rows, 2)], load_sem.at[7]
                ),
            ]
            for load in loads:
                load.start()
            for load in loads:
                load.wait()
            weight = cour_ref[v]
            lat_off, lon_off = off_ref[:, 0:1], off_ref[:, 1:2]

            def one(i):
                row = pad[i + 2]
                centre = row[:, rim : rim + lons]
                for step in (-2, -1, 1, 2):
                    row = jnp.where(lat_off == step, pad[i + 2 - step], row)
                moved = row[:, rim : rim + lons]
                for step in (-2, -1, 1, 2):
                    rolled = pltpu.roll(row, step % wide, 1)[:, rim : rim + lons]
                    moved = jnp.where(lon_off == step, rolled, moved)
                mixed = (1.0 - weight) * centre + weight * moved
                moved_buf[v, i] = mixed.astype(bf16)

            def pair(i, carry):
                one(2 * i)
                one(2 * i + 1)
                return carry

            lax.fori_loop(0, rows // 2, pair, 0)
            onward(v).start()

        def onward(v):
            return remote(
                moved_buf.at[v], prev.at[:, v], tm_send.at[v], tm_recv.at[v],
                (tm + 1) % n_tm, la, lo,
            )

        def correlate(k):
            def smooth_tile(i, carry):
                at_rows = at(i // (width // lon_tile), row_tile)
                at_lons = at(i % (width // lon_tile), lon_tile)
                smooth[at_rows, at_lons] = lax.dot_general(
                    whole[k, at_rows, :], table[at_lons, :], (((1,), (1,)), ((), ())),
                    preferred_element_type=jnp.float32,
                ).astype(bf16)
                return carry

            lax.fori_loop(0, (lats // row_tile) * (width // lon_tile), smooth_tile, 0)
            if k == 0:
                each_other(n_tm * n_lon, tm * n_lon + lo, lambda s: strip_arrival(s).wait_recv())

            def tile(i, carry):
                peer = (me + group // 2 + i) % group
                at_rows, at_lons = at(peer // n_lon, rows), at(peer % n_lon, lons)
                whole[k, at_rows, at_lons] = jnp.dot(
                    lat_table[at_rows, :], smooth[:, at_lons],
                    preferred_element_type=jnp.float32,
                ).astype(bf16)
                pl.when(peer != me)(lambda: homeward(k, peer, me).start())
                return carry

            lax.fori_loop(0, group, tile, 0)
            own_back(k).start()

        send_out(0)
        for load in own_tables():
            load.start()
        each_other(n_lat, la, lambda p: lat_share(p, la).start())
        each_other(n_lon, lo, lambda p: lon_share(p, lo).start())
        half = nvar // 2
        for v in range(half):
            advect(v)
        for k in range(1, rounds):
            send_out(k)
        for load in own_tables():
            load.wait()
        each_other(n_lat, la, lambda s: lat_share(s, s).wait_recv())
        each_other(n_tm * n_lon, tm * n_lon + lo, lambda p: strip_share(p, tm * n_lon + lo).start())
        for v in range(half, nvar):
            advect(v)
        each_other(n_lon, lo, lambda s: lon_share(s, s).wait_recv())
        for k in range(rounds):
            own(k).wait()
            each_other(group, me, lambda s: outward(k, s, s).wait_recv())
            correlate(k)
        each_other(n_lat, la, lambda p: lat_share(p, la).wait_send())
        each_other(n_lon, lo, lambda p: lon_share(p, lo).wait_send())
        each_other(
            n_tm * n_lon, tm * n_lon + lo, lambda p: strip_share(p, tm * n_lon + lo).wait_send()
        )
        for v in range(nvar):
            onward(v).wait()
        for k in range(rounds):
            own_back(k).wait()
            each_other(group, me, lambda p: outward(k, p, me).wait_send())
            each_other(group, me, lambda p: homeward(k, p, me).wait_send())
            each_other(group, me, lambda s: homeward(k, s, s).wait_recv())

    hbm = pl.BlockSpec(memory_space=pl.ANY)
    dma = pltpu.SemaphoreType.DMA
    n_strips = n_tm * n_lon
    return pl.pallas_call(
        kernel,
        in_specs=[
            pl.BlockSpec(memory_space=pltpu.VMEM),
            pl.BlockSpec(memory_space=pltpu.SMEM),
        ] + [hbm] * 8,
        out_specs=[hbm, hbm],
        out_shape=[
            jax.ShapeDtypeStruct((nvar * levels, rows, lons), bf16),
            jax.ShapeDtypeStruct((rows, nvar, levels, lons), bf16),
        ],
        scratch_shapes=[
            pltpu.VMEM((nvar * levels, rows, lons), bf16),
            pltpu.VMEM((rows, levels, lons), bf16),
            pltpu.VMEM((rounds, lats, width), bf16),
            pltpu.VMEM((width, width), bf16),
            pltpu.VMEM((lats, lats), bf16),
            pltpu.VMEM((lats, width), bf16),
            pltpu.VMEM((rows + 4, levels, wide), jnp.float32),
            pltpu.VMEM((nvar, rows, levels, lons), bf16),
            dma((8,)), dma((2 * rounds,)),
            dma((n_lon,)), dma((n_lon,)), dma((n_lat,)), dma((n_lat,)),
            dma((n_strips,)), dma((n_strips,)),
            dma((rounds, group)), dma((rounds, group)),
            dma((rounds, group)), dma((rounds, group)),
            dma((nvar,)), dma((nvar,)),
        ],
        compiler_params=pltpu.CompilerParams(
            vmem_limit_bytes=LIMIT, collective_id=0, has_side_effects=True
        ),
        cost_estimate=cost(2 * rounds * lats * width * (lats + width), 12 * control.size),
        name="exchange",
    )(offsets.T, courant, control, increments, low, high, below, above, lon_corr, lat_corr)


def whole_fields(control, deviations, increments, lon_corr, lat_corr, offsets, courant):
    rows, _, nvar, levels, lons = control.shape
    flat = (rows, nvar, levels, lons)
    control, deviations, increments = (
        x.reshape(flat) for x in (control, deviations, increments)
    )
    rims = widen(increments, 128)
    correlated, previous = exchange(
        control, increments, *rims, lon_corr, lat_corr, offsets, courant
    )
    correlated = correlated.reshape(nvar, levels, rows, lons)
    out = residual(increments, deviations, previous, correlated, 0, nvar, None)
    return out.reshape(rows, 1, nvar, levels, lons)


def body(control, deviations, increments, lon_corr, lat_corr, offsets, courant):
    rows, slots, nvar, levels, lons = control.shape
    group = lax.axis_size("lat") * lax.axis_size("lon")
    sharers = lax.axis_size("tm") * lax.axis_size("lon")
    arrays = (control, deviations, increments, lon_corr, lat_corr, offsets, courant)
    fits = (
        slots == 1
        and (nvar * levels) % group == 0
        and group % levels == 0
        and rows % 16 == 0
        and lons % 128 == 0
        and lat_corr.shape[1] % (128 * sharers) == 0
    )
    return whole_fields(*arrays) if fits else lat_columns(*arrays)


def solution(mesh):
    in_specs = (
        P("lat", "tm", None, None, "lon"),
        P("lat", "tm", None, None, "lon"),
        P("lat", "tm", None, None, "lon"),
        P("lon", None),
        P("lat", None),
        P(),
        P(),
    )
    out_specs = P("lat", "tm", None, None, "lon")
    return jax.shard_map(body, mesh=mesh, in_specs=in_specs, out_specs=out_specs, check_vma=False)
```

```python
import jax
import jax.numpy as jnp
from jax import lax
from jax.experimental import pallas as pl
from jax.experimental.pallas import tpu as pltpu
from jax.sharding import PartitionSpec as P


def with_halo(block, sides, width, periodic):
    for axis, dim in sides:
        count = lax.axis_size(axis)
        forward = [(i, i + 1) for i in range(count - 1)]
        if periodic:
            forward.append((count - 1, 0))
        backward = [(target, source) for source, target in forward]
        low = lax.ppermute(
            lax.slice_in_dim(block, block.shape[dim] - width, None, axis=dim), axis, forward
        )
        high = lax.ppermute(lax.slice_in_dim(block, 0, width, axis=dim), axis, backward)
        block = jnp.concatenate([low, block, high], axis=dim)
    return block


def from_behind(value, axis, steps):
    count = lax.axis_size(axis)
    initial, last = (max(0, -steps), min(count, count - steps))
    return lax.ppermute(value, axis, [(source, source + steps) for source in range(initial, last)])


def advect(field_now, offsets, courant):
    widened = with_halo(field_now.astype(jnp.bfloat16), (("lon", 4),), 2, True).astype(
        field_now.dtype
    )
    padded = with_halo(widened.astype(jnp.bfloat16), (("lat", 0),), 2, False).astype(widened.dtype)
    lat_count = field_now.shape[0]
    lon_count = field_now.shape[4]
    displaced_all = []
    for level_idx in range(field_now.shape[3]):
        one_level = padded[:, :, :, level_idx, :]
        displaced = lax.dynamic_slice_in_dim(one_level, 2 - offsets[0, level_idx], lat_count, 0)
        displaced = lax.dynamic_slice_in_dim(displaced, 2 - offsets[1, level_idx], lon_count, 3)
        displaced_all.append(displaced)
    shifted = jnp.stack(displaced_all, axis=3)
    blending = courant.reshape(1, 1, -1, 1, 1)
    return (1.0 - blending) * field_now + blending * shifted


def lat_columns(control, deviations, increments, lon_corr, lat_corr, offsets, courant):
    lat_count = control.shape[0]
    lon_count = control.shape[4]
    flat_rows = control.reshape(-1, lon_count)
    smoothed = lax.dot_general(
        lax.all_gather(flat_rows, "lon", axis=1, tiled=True),
        lon_corr,
        (((1,), (1,)), ((), ())),
        preferred_element_type=jnp.float32,
    )
    halfway = smoothed.astype(jnp.bfloat16).reshape(lat_count, -1)
    full_table = lax.all_gather(lat_corr, "lat", axis=0, tiled=True)
    columns_all = lax.all_to_all(halfway, "lat", split_axis=1, concat_axis=0, tiled=True)
    product = jnp.dot(full_table, columns_all, preferred_element_type=jnp.float32)
    correlated = lax.all_to_all(product, "lat", split_axis=0, concat_axis=1, tiled=True)
    forcing = deviations * correlated.reshape(control.shape)
    evolved = advect(increments, offsets, courant)
    carried = from_behind(evolved, "tm", 1)
    previous = jnp.concatenate([carried, evolved[:, :-1]], axis=1)
    return increments - previous - forcing


LIMIT = 60 * 1024 * 1024


def cost(flops, nbytes):
    return pl.CostEstimate(flops=flops, bytes_accessed=nbytes, transcendentals=0)


def row_block(rows, largest):
    block = min(rows, largest)
    while rows % block:
        block -= 16
    return block


def residual(increments, deviations, previous, correlated, first, count, filled):
    rows, nvar, levels, lons = increments.shape
    block = row_block(rows, 32)

    def kernel(inc_ref, dev_ref, prev_ref, corr_ref, *others):
        out_ref = others[-1]
        corr = jnp.swapaxes(corr_ref[0].astype(jnp.float32), 0, 1)
        has_past = lax.axis_index("tm") > 0
        previous = jnp.where(has_past, prev_ref[:, 0].astype(jnp.float32), 0.0)
        out_ref[:, 0] = (
            inc_ref[:, 0] - previous - dev_ref[:, 0] * corr
        )

    spec = pl.BlockSpec((block, 1, levels, lons), lambda v, r: (r, first + v, 0, 0))
    in_specs = [spec] * 3 + [
        pl.BlockSpec((1, levels, block, lons), lambda v, r: (v, 0, r, 0))
    ]
    operands = [increments, deviations, previous, correlated]
    aliases = {}
    if filled is not None:
        in_specs.append(pl.BlockSpec(memory_space=pl.ANY))
        operands.append(filled)
        aliases = {4: 0}
    return pl.pallas_call(
        kernel,
        grid=(count, rows // block),
        in_specs=in_specs,
        out_specs=spec,
        out_shape=jax.ShapeDtypeStruct(increments.shape, jnp.float32),
        input_output_aliases=aliases,
        compiler_params=pltpu.CompilerParams(vmem_limit_bytes=LIMIT),
        cost_estimate=cost(6 * count * levels * rows * lons, 16 * count * levels * rows * lons),
        name="residual",
    )(*operands)


def exchange(control, increments, lon_corr, lat_corr, offsets, courant):
    rows, nvar, levels, lons = control.shape
    n_tm, n_lat, n_lon = (lax.axis_size(axis) for axis in ("tm", "lat", "lon"))
    group = n_lat * n_lon
    rounds = nvar * levels // group
    vars_each = nvar // rounds
    lats, width = n_lat * rows, n_lon * lons
    rim = 128
    wide = lons + 2 * rim
    strip = lat_corr.shape[1] // (n_tm * n_lon)
    row_tile = row_block(lats, 256)
    lon_tile = row_block(width, 512)
    bf16 = jnp.bfloat16

    def kernel(
        off_ref, cour_ref, ctl, inc, lonc, latc,
        corr, prev, low_ref, high_ref, below_ref, above_ref,
        stage, ctl_buf, whole, table, lat_table, smooth, pad, moved_buf,
        load_sem, self_sem, lon_send, lon_recv, lat_send, lat_recv, tab_send, tab_recv,
        out_send, out_recv, back_send, back_recv, tm_send, tm_recv,
        side_send, side_recv, edge_send, edge_recv,
    ):
        tm, la, lo = (lax.axis_index(axis) for axis in ("tm", "lat", "lon"))
        me = la * n_lon + lo
        strip_at = (tm * n_lon + lo) * strip

        def at(index, size):
            return pl.ds(pl.multiple_of(index * size, size), size)

        def remote(src, dst, send, recv, tm_to, lat_to, lon_to):
            return pltpu.make_async_remote_copy(
                src_ref=src, dst_ref=dst, send_sem=send, recv_sem=recv,
                device_id=(tm_to, lat_to, lon_to), device_id_type=pl.DeviceIdType.MESH,
            )

        def each_other(count, mine, do):
            def step(i, carry):
                pl.when(i != mine)(lambda: do(i))
                return carry

            lax.fori_loop(0, count, step, 0)

        barrier = pltpu.get_barrier_semaphore()

        def greet(tm_to, peer):
            pl.semaphore_signal(
                barrier, inc=1, device_id=(tm_to, peer // n_lon, peer % n_lon),
                device_id_type=pl.DeviceIdType.MESH,
            )

        each_other(group, me, lambda peer: greet(tm, peer))
        for lon_to in range(n_lon):
            each_other(n_tm, tm, lambda other: greet(other, la * n_lon + lon_to))
        pl.semaphore_wait(barrier, group - 1 + (n_tm - 1) * n_lon)

        left, right = (lo + n_lon - 1) % n_lon, (lo + 1) % n_lon
        centre_lanes, low_lanes, high_lanes = (
            pl.ds(rim, lons), pl.ds(0, rim), pl.ds(rim + lons, rim)
        )

        def sides():
            return (
                remote(
                    inc.at[:, :, :, pl.ds(lons - rim, rim)], low_ref,
                    side_send.at[0], side_recv.at[0], tm, la, right,
                ),
                remote(
                    inc.at[:, :, :, pl.ds(0, rim)], high_ref,
                    side_send.at[1], side_recv.at[1], tm, la, left,
                ),
            )

        def edges(way):
            first, dst, lat_to = ((rows - 2, below_ref, la + 1), (0, above_ref, la - 1))[way]
            parts = (
                (pl.ds(0, lons), centre_lanes, lo),
                (pl.ds(lons - rim, rim), low_lanes, right),
                (pl.ds(0, rim), high_lanes, left),
            )
            return [
                remote(
                    inc.at[pl.ds(first, 2), :, :, src_lanes], dst.at[:, :, :, dst_lanes],
                    edge_send.at[3 * way + i], edge_recv.at[3 * way + i], tm, lat_to, lon_to,
                )
                for i, (src_lanes, dst_lanes, lon_to) in enumerate(parts)
            ]

        has_below, has_above = la > 0, la < n_lat - 1

        def start_rims():
            for copy in sides():
                copy.start()
            for way, may_send in enumerate((has_above, has_below)):

                @pl.when(may_send)
                def _():
                    for copy in edges(way):
                        copy.start()

        def wait_rims():
            for copy in sides():
                copy.wait()
            for way, (may_send, may_get) in enumerate(
                ((has_above, has_below), (has_below, has_above))
            ):

                @pl.when(may_send)
                def _():
                    for copy in edges(way):
                        copy.wait_send()

                @pl.when(may_get)
                def _():
                    for copy in edges(way):
                        copy.wait_recv()

        def outward(k, peer, origin):
            return remote(
                stage.at[k * group + peer],
                whole.at[k, at(origin // n_lon, rows), at(origin % n_lon, lons)],
                out_send.at[k, peer], out_recv.at[k, origin],
                tm, peer // n_lon, peer % n_lon,
            )

        def homeward(k, peer, origin):
            return remote(
                whole.at[k, at(peer // n_lon, rows), at(peer % n_lon, lons)],
                corr.at[k * group + origin],
                back_send.at[k, peer], back_recv.at[k, origin],
                tm, peer // n_lon, peer % n_lon,
            )

        def lon_share(lon_to, origin):
            return remote(
                lonc, table.at[at(origin, lons)],
                lon_send.at[lon_to], lon_recv.at[origin], tm, la, lon_to,
            )

        def lat_share(lat_to, origin):
            columns = at(tm * n_lon + lo, strip)
            return remote(
                latc.at[:, columns], lat_table.at[at(origin, rows), columns],
                lat_send.at[lat_to], lat_recv.at[origin], tm, lat_to, lo,
            )

        def strip_share(other, origin):
            return remote(
                lat_table.at[:, at(tm * n_lon + lo, strip)],
                lat_table.at[:, at(tm * n_lon + lo, strip)],
                tab_send.at[other], tab_recv.at[origin], other // n_lon, la, other % n_lon,
            )

        def strip_arrival(origin):
            return remote(
                lat_table.at[:, at(origin, strip)], lat_table.at[:, at(origin, strip)],
                tab_send.at[origin], tab_recv.at[origin], origin // n_lon, la, origin % n_lon,
            )

        def own(k):
            return pltpu.make_async_copy(
                stage.at[k * group + me], whole.at[k, at(la, rows), at(lo, lons)],
                self_sem.at[k],
            )

        def own_back(k):
            return pltpu.make_async_copy(
                whole.at[k, at(la, rows), at(lo, lons)], corr.at[k * group + me],
                self_sem.at[rounds + k],
            )

        def own_tables():
            columns = at(tm * n_lon + lo, strip)
            return (
                pltpu.make_async_copy(lonc, table.at[at(lo, lons)], load_sem.at[0]),
                pltpu.make_async_copy(
                    latc.at[:, columns], lat_table.at[at(la, rows), columns], load_sem.at[1]
                ),
            )

        def send_out(k):
            far = (me * vars_each // group + vars_each // 2) % vars_each
            for t in range(vars_each):
                local = (far + t) % vars_each
                load = pltpu.make_async_copy(
                    ctl.at[:, k * vars_each + local], ctl_buf, load_sem.at[2]
                )
                load.start()
                load.wait()

                def turn(r, carry):
                    part = ctl_buf[pl.ds(r * 16, 16)].astype(jnp.float32)
                    first = (k * vars_each + local) * levels
                    stage[pl.ds(first, levels), pl.ds(r * 16, 16), :] = jnp.swapaxes(
                        part, 0, 1
                    ).astype(bf16)
                    return carry

                lax.fori_loop(0, rows // 16, turn, 0)

                def send(l, carry):
                    peer = local * levels + l
                    pl.when(peer != me)(lambda: outward(k, peer, me).start())
                    return carry

                lax.fori_loop(0, levels, send, 0)
            own(k).start()

        def advect(v):
            body_rows = pl.ds(2, rows)
            loads = [
                pltpu.make_async_copy(
                    inc.at[:, v], pad.at[body_rows, :, pl.ds(rim, lons)], load_sem.at[3]
                ),
                pltpu.make_async_copy(
                    low_ref.at[:, v], pad.at[body_rows, :, pl.ds(0, rim)], load_sem.at[4]
                ),
                pltpu.make_async_copy(
                    high_ref.at[:, v], pad.at[body_rows, :, pl.ds(rim + lons, rim)],
                    load_sem.at[5],
                ),
            ]
            for load in loads:
                load.start()
            for present, ref, first, sem in (
                (has_below, below_ref, 0, 6), (has_above, above_ref, 2 + rows, 7)
            ):

                @pl.when(present)
                def _():
                    load = pltpu.make_async_copy(
                        ref.at[:, v], pad.at[pl.ds(first, 2)], load_sem.at[sem]
                    )
                    load.start()
                    load.wait()

                @pl.when(jnp.logical_not(present))
                def _():
                    pad[pl.ds(first, 2)] = jnp.zeros((2, levels, wide), jnp.float32)

            for load in loads:
                load.wait()
            weight = cour_ref[v]
            lat_off, lon_off = off_ref[:, 0:1], off_ref[:, 1:2]

            def one(i):
                row = pad[i + 2]
                centre = row[:, rim : rim + lons]
                for step in (-2, -1, 1, 2):
                    row = jnp.where(lat_off == step, pad[i + 2 - step], row)
                moved = row[:, rim : rim + lons]
                for step in (-2, -1, 1, 2):
                    rolled = pltpu.roll(row, step % wide, 1)[:, rim : rim + lons]
                    moved = jnp.where(lon_off == step, rolled, moved)
                mixed = (1.0 - weight) * centre + weight * moved
                moved_buf[v, i] = mixed.astype(bf16)

            def pair(i, carry):
                one(2 * i)
                one(2 * i + 1)
                return carry

            lax.fori_loop(0, rows // 2, pair, 0)
            onward(v).start()

        def onward(v):
            return remote(
                moved_buf.at[v], prev.at[:, v], tm_send.at[v], tm_recv.at[v],
                (tm + 1) % n_tm, la, lo,
            )

        def correlate(k):
            def smooth_tile(i, carry):
                at_rows = at(i // (width // lon_tile), row_tile)
                at_lons = at(i % (width // lon_tile), lon_tile)
                smooth[at_rows, at_lons] = lax.dot_general(
                    whole[k, at_rows, :], table[at_lons, :], (((1,), (1,)), ((), ())),
                    preferred_element_type=jnp.float32,
                ).astype(bf16)
                return carry

            lax.fori_loop(0, (lats // row_tile) * (width // lon_tile), smooth_tile, 0)
            if k == 0:
                each_other(n_tm * n_lon, tm * n_lon + lo, lambda s: strip_arrival(s).wait_recv())

            def tile(i, carry):
                peer = (me + group // 2 + i) % group
                at_rows, at_lons = at(peer // n_lon, rows), at(peer % n_lon, lons)
                whole[k, at_rows, at_lons] = jnp.dot(
                    lat_table[at_rows, :], smooth[:, at_lons],
                    preferred_element_type=jnp.float32,
                ).astype(bf16)
                pl.when(peer != me)(lambda: homeward(k, peer, me).start())
                return carry

            lax.fori_loop(0, group, tile, 0)
            own_back(k).start()

        start_rims()
        send_out(0)
        for load in own_tables():
            load.start()
        each_other(n_lat, la, lambda p: lat_share(p, la).start())
        each_other(n_lon, lo, lambda p: lon_share(p, lo).start())
        half = nvar // 2
        wait_rims()
        for v in range(half):
            advect(v)
        for k in range(1, rounds):
            send_out(k)
        for load in own_tables():
            load.wait()
        each_other(n_lat, la, lambda s: lat_share(s, s).wait_recv())
        each_other(n_tm * n_lon, tm * n_lon + lo, lambda p: strip_share(p, tm * n_lon + lo).start())
        for v in range(half, nvar):
            advect(v)
        each_other(n_lon, lo, lambda s: lon_share(s, s).wait_recv())
        for k in range(rounds):
            own(k).wait()
            each_other(group, me, lambda s: outward(k, s, s).wait_recv())
            correlate(k)
        each_other(n_lat, la, lambda p: lat_share(p, la).wait_send())
        each_other(n_lon, lo, lambda p: lon_share(p, lo).wait_send())
        each_other(
            n_tm * n_lon, tm * n_lon + lo, lambda p: strip_share(p, tm * n_lon + lo).wait_send()
        )
        for v in range(nvar):
            onward(v).wait()
        for k in range(rounds):
            own_back(k).wait()
            each_other(group, me, lambda p: outward(k, p, me).wait_send())
            each_other(group, me, lambda p: homeward(k, p, me).wait_send())
            each_other(group, me, lambda s: homeward(k, s, s).wait_recv())

    hbm = pl.BlockSpec(memory_space=pl.ANY)
    dma = pltpu.SemaphoreType.DMA
    n_strips = n_tm * n_lon
    return pl.pallas_call(
        kernel,
        in_specs=[
            pl.BlockSpec(memory_space=pltpu.VMEM),
            pl.BlockSpec(memory_space=pltpu.SMEM),
        ] + [hbm] * 4,
        out_specs=[hbm] * 6,
        out_shape=[
            jax.ShapeDtypeStruct((nvar * levels, rows, lons), bf16),
            jax.ShapeDtypeStruct((rows, nvar, levels, lons), bf16),
            jax.ShapeDtypeStruct((rows, nvar, levels, rim), jnp.float32),
            jax.ShapeDtypeStruct((rows, nvar, levels, rim), jnp.float32),
            jax.ShapeDtypeStruct((2, nvar, levels, wide), jnp.float32),
            jax.ShapeDtypeStruct((2, nvar, levels, wide), jnp.float32),
        ],
        scratch_shapes=[
            pltpu.VMEM((nvar * levels, rows, lons), bf16),
            pltpu.VMEM((rows, levels, lons), bf16),
            pltpu.VMEM((rounds, lats, width), bf16),
            pltpu.VMEM((width, width), bf16),
            pltpu.VMEM((lats, lats), bf16),
            pltpu.VMEM((lats, width), bf16),
            pltpu.VMEM((rows + 4, levels, wide), jnp.float32),
            pltpu.VMEM((nvar, rows, levels, lons), bf16),
            dma((8,)), dma((2 * rounds,)),
            dma((n_lon,)), dma((n_lon,)), dma((n_lat,)), dma((n_lat,)),
            dma((n_strips,)), dma((n_strips,)),
            dma((rounds, group)), dma((rounds, group)),
            dma((rounds, group)), dma((rounds, group)),
            dma((nvar,)), dma((nvar,)),
            dma((2,)), dma((2,)), dma((6,)), dma((6,)),
        ],
        compiler_params=pltpu.CompilerParams(
            vmem_limit_bytes=LIMIT, collective_id=0, has_side_effects=True
        ),
        cost_estimate=cost(2 * rounds * lats * width * (lats + width), 12 * control.size),
        name="exchange",
    )(offsets.T, courant, control, increments, lon_corr, lat_corr)[:2]


def whole_fields(control, deviations, increments, lon_corr, lat_corr, offsets, courant):
    rows, _, nvar, levels, lons = control.shape
    flat = (rows, nvar, levels, lons)
    control, deviations, increments = (
        x.reshape(flat) for x in (control, deviations, increments)
    )
    correlated, previous = exchange(
        control, increments, lon_corr, lat_corr, offsets, courant
    )
    correlated = correlated.reshape(nvar, levels, rows, lons)
    out = residual(increments, deviations, previous, correlated, 0, nvar, None)
    return out.reshape(rows, 1, nvar, levels, lons)


def body(control, deviations, increments, lon_corr, lat_corr, offsets, courant):
    rows, slots, nvar, levels, lons = control.shape
    group = lax.axis_size("lat") * lax.axis_size("lon")
    sharers = lax.axis_size("tm") * lax.axis_size("lon")
    arrays = (control, deviations, increments, lon_corr, lat_corr, offsets, courant)
    fits = (
        slots == 1
        and lax.axis_size("lat") > 1
        and lax.axis_size("lon") > 1
        and lax.axis_size("tm") > 1
        and (nvar * levels) % group == 0
        and group % levels == 0
        and rows % 16 == 0
        and lons % 128 == 0
        and lat_corr.shape[1] % (128 * sharers) == 0
    )
    return whole_fields(*arrays) if fits else lat_columns(*arrays)


def solution(mesh):
    in_specs = (
        P("lat", "tm", None, None, "lon"),
        P("lat", "tm", None, None, "lon"),
        P("lat", "tm", None, None, "lon"),
        P("lon", None),
        P("lat", None),
        P(),
        P(),
    )
    out_specs = P("lat", "tm", None, None, "lon")
    return jax.shard_map(body, mesh=mesh, in_specs=in_specs, out_specs=out_specs, check_vma=False)
```
